32 devices in a mesh: atoms: 16 (over z, x, core), width: 2 (over y).
Axes of the slice: x: 2, y: 2, z: 4, core: 2. Of those that a mesh axis runs over, the one named last changes fastest.
Arguments:
- tokens: bfloat16 [2048, 8192], P('atoms', 'width'), may hold values from -6 to 6
- dec_bias: float32 [8192], P('width'), may hold values from -3 to 3
- encoder: bfloat16 [2048, 8192], P('atoms', 'width'), may hold values from -1.5 to 1.5
- enc_bias: float32 [2048], P('atoms'), may hold values from -24 to 24
- decoder: bfloat16 [2048, 8192], P('atoms', 'width'), may hold values from -0.25 to 0.25
- atom_ids: int32 [2048, 16], P('atoms'), may hold values from 0 to 2047, as said below
- block_count: int32 [16], P('atoms'), may hold values from 1 to 2, as said below
Outputs:
- residual: bfloat16 [2048, 8192], P('atoms', 'width')
- encoder_grad: bfloat16 [2048, 8192], P('atoms', 'width')
- decoder_grad: bfloat16 [2048, 8192], P('atoms', 'width')
- bias_grad: float32 [2048], P('atoms')
The draws below stay inside these ranges and needn't reach their ends.
Inputs may be any that keep to these rules, and one draw needn't show every extreme that they name: atom_ids[t, 2g] and atom_ids[t, 2g + 1] are two different atom slots of one owner o (slot // 128 = o), both below o * 128 + 64 block_count[o]; the 8 owners of one token differ. Of the 128 tokens of one index of atoms, at most 96 use any one owner, and in every draw some owner is used by exactly 96 tokens of every index of atoms. `block_count`: every draw has an owner with 2 live blocks and one with a single live block.
All inputs are finite; a program needn't handle non-finite values.
Results may differ from the reference program's by a relative error of at most 0.018.
Values may be sent and summed in bfloat16 or wider, within the bound.
A program may use at most 128 MiB of HBM per device.

```python
import math
import jax
import jax.numpy as jnp
from jax import lax

D = 8192
GROUPS = 8
BLOCK = 64
BLK_DEV = 2
ATOMS = 2048
TOK_DEV = 128
TOKENS = 2048
N_ATOMS = 16


def routing(key):
    base_key = jax.random.fold_in(key, 5)
    k_hot, k_count, k_full, k_low, k_src = jax.random.split(base_key, 5)
    all_owners = jnp.arange(N_ATOMS)
    counts = jax.random.randint(k_count, (N_ATOMS,), 1, BLK_DEV + 1)
    full_owner = jax.random.randint(k_full, (), 0, N_ATOMS)
    low_owner = (full_owner + jax.random.randint(k_low, (), 1, N_ATOMS)) % N_ATOMS
    counts = jnp.where(all_owners == full_owner, BLK_DEV, jnp.where(all_owners == low_owner, 1, counts))
    hot_owner = jax.random.randint(k_hot, (), 0, N_ATOMS)
    residues = N_ATOMS // GROUPS
    capacity = 3 * TOK_DEV * GROUPS // (2 * N_ATOMS)

    def one_source(source_key):
        k_perm, k_tok, k_first, k_shift = jax.random.split(source_key, 4)
        owner_order = jax.random.permutation(k_perm, N_ATOMS)
        hot_place = jnp.sum(jnp.where(owner_order == hot_owner, all_owners, 0))
        hot_res = hot_place % residues
        token_rank = jax.random.permutation(k_tok, TOK_DEV)
        other_res = (hot_res + 1 + (token_rank - capacity) % max(residues - 1, 1)) % residues
        residue = jnp.where(token_rank < capacity, hot_res, other_res)
        pick_index = residue[:, None] + residues * jnp.arange(GROUPS)[None, :]
        owner_of = owner_order[pick_index]
        live_atoms = counts[owner_of] * BLOCK
        first_atom = jax.random.randint(k_first, (TOK_DEV, GROUPS), 0, live_atoms)
        atom_shift = jax.random.randint(k_shift, (TOK_DEV, GROUPS), 1, live_atoms)
        second_atom = (first_atom + atom_shift) % live_atoms
        base_id = owner_of * (BLK_DEV * BLOCK)
        return jnp.stack([base_id + first_atom, base_id + second_atom], axis=2).reshape(TOK_DEV, 2 * GROUPS)
    chosen = jax.vmap(one_source)(jax.random.split(k_src, N_ATOMS))
    return (chosen.reshape(N_ATOMS * TOK_DEV, 2 * GROUPS).astype(jnp.int32), counts.astype(jnp.int32))


def draw_atom_ids(key, part):
    return routing(key)[0]


def draw_block_count(key, part):
    return routing(key)[1]


def draw_decoder(key, part):
    key_noise, key_rows, key_cols = jax.random.split(jax.random.fold_in(key, 11), 3)
    noise = jnp.clip(jax.random.normal(key_noise, (ATOMS, D), jnp.float32), -6.0, 6.0)
    row_scale = jnp.exp(jax.random.uniform(key_rows, (ATOMS, 1), jnp.float32, -1.15, 1.15))
    col_scale = jnp.exp(jax.random.uniform(key_cols, (1, D), jnp.float32, -1.15, 1.15))
    values = noise * row_scale * col_scale * (0.68 / jnp.sqrt(jnp.float32(D)))
    return jnp.clip(values, -0.25, 0.25).astype(jnp.bfloat16)


def levels(stream_key, shape, pieces, smallest, top_value):
    factor_of, own = 1.0, jax.random.fold_in(stream_key, 6)
    for dim, blocks in pieces:
        draws = jnp.exp(jax.random.uniform(jax.random.fold_in(own, dim), (blocks,), jnp.float32, smallest / len(pieces), top_value / len(pieces)))
        factor_of = factor_of * jnp.repeat(draws, shape[dim] // blocks).reshape([-1 if axis == dim else 1 for axis in range(len(shape))])
    return factor_of


def gaussian(stream_key, shape, scale, limit, pieces=(), kind=jnp.bfloat16):
    result = scale * jax.random.normal(stream_key, shape, jnp.float32)
    if pieces:
        result = result * levels(stream_key, shape, pieces, -0.22, 0.18)
    return jnp.clip(result, -limit, limit).astype(kind)


def setup_inputs(seed: int = 0) -> dict:
    key_list = jax.random.split(jax.random.key(seed), 8)
    tokens = gaussian(key_list[0], (TOKENS, D), 1.0, 6.0, ((0, 16), (1, 2)))
    dec_bias = gaussian(key_list[1], (D,), 0.5, 3.0, ((0, 2),), jnp.float32)
    encoder = gaussian(key_list[2], (ATOMS, D), 16 ** -0.5, 1.5, ((0, 16), (1, 2)))
    enc_bias = gaussian(key_list[3], (ATOMS,), 4.0, 24.0, ((0, 16),), jnp.float32)
    decoder = draw_decoder(jax.random.fold_in(key_list[7], 71), 0)
    atom_ids = draw_atom_ids(jax.random.fold_in(key_list[7], 71), 0)
    block_count = draw_block_count(jax.random.fold_in(key_list[7], 71), 0)
    return {"tokens": tokens, "dec_bias": dec_bias, "encoder": encoder, "enc_bias": enc_bias, "decoder": decoder, "atom_ids": atom_ids, "block_count": block_count}


coherence = 128.0
loss_grad = 1.0 / 32.0
epsilon = 1e-06

def rounded(value):
    return lax.optimization_barrier(value.astype(jnp.bfloat16))

def coherence_grad(rows, alive):
    raw_gram = jnp.dot(rows, rows.T, preferred_element_type=jnp.float32)
    norms = jnp.sqrt(jnp.diagonal(raw_gram) + epsilon)
    norm_pair = norms[:, None] * norms[None, :]
    cosine = raw_gram / norm_pair
    extent = rows.shape[0]
    on_diagonal = jnp.arange(extent)[:, None] == jnp.arange(extent)[None, :]
    coupled = jnp.where(on_diagonal, 0.0, alive[:, None] * alive[None, :] * cosine)
    spread = lax.optimization_barrier(jnp.sum(coupled * cosine, axis=1))
    diag_term = jnp.where(on_diagonal, (spread / (norms * norms))[:, None], 0.0)
    weights = (4.0 * coherence * (coupled / norm_pair - diag_term)).astype(jnp.bfloat16)
    return jnp.dot(weights, rows, preferred_element_type=jnp.float32)

def owner_grad(pair):
    return coherence_grad(pair[0], pair[1])

def reference(tokens, dec_bias, encoder, enc_bias, decoder, atom_ids, block_count):
    total, width = tokens.shape
    pick = atom_ids.shape[1]
    atoms_total = encoder.shape[0]
    centered = (tokens.astype(jnp.float32) - dec_bias).astype(jnp.bfloat16)
    block_rows = math.gcd(total, 256)

    def step(carry, index):
        enc_acc, dec_acc, bias_acc = carry
        start = index * block_rows
        cen_rows = lax.dynamic_slice_in_dim(centered, start, block_rows, 0)
        tok_rows = lax.dynamic_slice_in_dim(tokens, start, block_rows, 0)
        chosen = lax.dynamic_slice_in_dim(atom_ids, start, block_rows, 0)
        enc_rows = encoder[chosen].astype(jnp.float32)
        pre = jnp.einsum('td,tkd->tk', cen_rows.astype(jnp.float32), enc_rows) + enc_bias[chosen]
        act = rounded(pre).astype(jnp.float32)
        dec_rows = decoder[chosen].astype(jnp.float32)
        terms = act[:, :, None] * dec_rows
        decoded = rounded(lax.optimization_barrier(jnp.sum(terms.reshape(block_rows, pick // 2, 2, width), axis=2))).astype(jnp.float32)
        resid = rounded(lax.optimization_barrier(jnp.sum(decoded, axis=1)) + dec_bias - tok_rows.astype(jnp.float32))
        resid_wide = resid.astype(jnp.float32)
        act_grad = jnp.einsum('td,tkd->tk', resid_wide, dec_rows) * loss_grad
        flat_ids = chosen.reshape(-1)
        enc_terms = (rounded(act_grad).astype(jnp.float32)[:, :, None] * cen_rows.astype(jnp.float32)[:, None, :]).reshape(-1, width)
        dec_terms = (act[:, :, None] * resid_wide[:, None, :]).reshape(-1, width)
        enc_acc = enc_acc.at[flat_ids].add(enc_terms)
        dec_acc = dec_acc.at[flat_ids].add(dec_terms)
        bias_acc = bias_acc.at[flat_ids].add(act_grad.reshape(-1))
        return ((enc_acc, dec_acc, bias_acc), resid)
    start_state = (jnp.zeros((atoms_total, width), jnp.float32), jnp.zeros((atoms_total, width), jnp.float32), jnp.zeros((atoms_total,), jnp.float32))
    (enc_acc, dec_acc, bias_acc), resid_blocks = lax.scan(step, start_state, jnp.arange(total // block_rows, dtype=jnp.int32))
    residual = resid_blocks.reshape(total, width)
    owners = block_count.shape[0]
    atom_dev = atoms_total // owners
    alive = (jnp.arange(atom_dev)[None, :] < block_count[:, None] * BLOCK).astype(jnp.float32)
    penalty = lax.map(owner_grad, (decoder.reshape(owners, atom_dev, width), alive))
    encoder_grad = enc_acc.astype(jnp.bfloat16)
    decoder_grad = (dec_acc * loss_grad + penalty.reshape(atoms_total, width)).astype(jnp.bfloat16)
    return (residual, encoder_grad, decoder_grad, bias_acc)
```

```python
import functools

import jax
import jax.numpy as jnp
from jax import lax
from jax.experimental import pallas as pl
from jax.experimental.pallas import tpu as pltpu
from jax.sharding import PartitionSpec as P

BLOCK = 64


coherence = 128.0
loss_grad = 1.0 / 32.0
epsilon = 1e-06


def coherence_weights(raw_rows, norm_rows, norm_all, alive_rows, alive_all):
    row_total, extent = raw_rows.shape
    row_ids = jnp.arange(row_total)[:, None]
    col_ids = jnp.arange(extent)[None, :]
    norm_pair = norm_rows[:, None] * norm_all[None, :]
    cosine = raw_rows / norm_pair
    on_diagonal = row_ids == col_ids
    coupled = jnp.where(on_diagonal, 0.0, alive_rows[:, None] * alive_all[None, :] * cosine)
    spread = jnp.sum(coupled * cosine, axis=1)
    diag_term = jnp.where(on_diagonal, (spread / (norm_rows * norm_rows))[:, None], 0.0)
    return (4.0 * coherence * (coupled / norm_pair - diag_term)).astype(jnp.bfloat16)


def picked_pair(table, hit_a, hit_b):
    first_pick = jnp.sum(jnp.where(hit_a, table, 0.0), axis=1)
    second_pick = jnp.sum(jnp.where(hit_b, table, 0.0), axis=1)
    return (first_pick, second_pick)


def dispatched(tokens, dec_bias, encoder, enc_bias, decoder, atom_ids, block_count):
    tok_dev, width_shard = tokens.shape
    atom_dev = encoder.shape[0]
    owner_total = lax.axis_size("atoms")
    pair_total = atom_ids.shape[1] // 2
    capacity = 3 * tok_dev * pair_total // (2 * owner_total)
    slot_total = owner_total * capacity
    contract = (((1,), (1,)), ((), ()))
    contract_rows = (((0,), (0,)), ((), ()))
    centered = (tokens.astype(jnp.float32) - dec_bias).astype(jnp.bfloat16)
    pair_ids = atom_ids.reshape(tok_dev * pair_total, 2)
    owner_of = pair_ids[:, 0] // atom_dev
    local_atom = pair_ids % atom_dev
    member = (owner_of[:, None] == jnp.arange(owner_total)[None, :]).astype(jnp.int32)
    before = jnp.cumsum(member, axis=0) - member
    slot_of = owner_of * capacity + jnp.sum(before * member, axis=1)
    source_tok = jnp.arange(tok_dev * pair_total) // pair_total
    outgoing = (
        jnp.zeros((slot_total, width_shard), jnp.bfloat16).at[slot_of].set(centered[source_tok])
    )
    slot_tags = jnp.concatenate([local_atom, source_tok[:, None]], axis=1)
    tag_out = jnp.full((slot_total, 3), -1, jnp.int32).at[slot_of].set(slot_tags)
    incoming = lax.all_to_all(outgoing, "atoms", split_axis=0, concat_axis=0, tiled=True)
    tag_in = lax.all_to_all(tag_out, "atoms", split_axis=0, concat_axis=0, tiled=True)
    columns = jnp.arange(atom_dev)[None, :]
    hit_a = tag_in[:, 0:1] == columns
    hit_b = tag_in[:, 1:2] == columns
    scores = lax.dot_general(incoming, encoder, contract, preferred_element_type=jnp.float32)
    scores = lax.psum(scores.astype(jnp.bfloat16), "width").astype(jnp.float32)
    pre_a, pre_b = picked_pair(scores, hit_a, hit_b)
    bias_a, bias_b = picked_pair(enc_bias[None, :], hit_a, hit_b)
    act_a = (pre_a + bias_a).astype(jnp.bfloat16)
    act_b = (pre_b + bias_b).astype(jnp.bfloat16)
    zero_low = jnp.zeros((), jnp.bfloat16)
    act_table = jnp.where(hit_a, act_a[:, None], zero_low) + jnp.where(
        hit_b, act_b[:, None], zero_low
    )
    decoded = jnp.dot(act_table, decoder, preferred_element_type=jnp.float32).astype(jnp.bfloat16)
    returned = lax.all_to_all(decoded, "atoms", split_axis=0, concat_axis=0, tiled=True)
    own_terms = returned[slot_of].reshape(tok_dev, pair_total, width_shard).astype(jnp.float32)
    residual = (jnp.sum(own_terms, axis=1) + dec_bias - tokens.astype(jnp.float32)).astype(
        jnp.bfloat16
    )
    token_of_slot = jnp.maximum(tag_in[:, 2], 0)
    piece = lax.all_gather(residual, "atoms", axis=0, tiled=True)
    rows = piece.shape[0]
    src_count = rows // tok_dev
    offset = jnp.arange(src_count * capacity) // capacity * tok_dev
    picked = piece[token_of_slot + offset]
    back_scores = lax.dot_general(picked, decoder, contract, preferred_element_type=jnp.float32)
    back_scores = lax.psum(back_scores.astype(jnp.bfloat16), "width").astype(jnp.float32)
    grad_a, grad_b = picked_pair(back_scores, hit_a, hit_b)
    dact_a = grad_a * loss_grad
    dact_b = grad_b * loss_grad
    dact_table = jnp.where(hit_a, dact_a[:, None], 0.0) + jnp.where(hit_b, dact_b[:, None], 0.0)
    bias_grad = jnp.sum(dact_table, axis=0)
    encoder_grad = lax.dot_general(
        dact_table.astype(jnp.bfloat16), incoming, contract_rows, preferred_element_type=jnp.float32
    ).astype(jnp.bfloat16)
    fitted = (
        lax.dot_general(act_table, picked, contract_rows, preferred_element_type=jnp.float32)
        * loss_grad
    )
    raw_gram = lax.dot_general(decoder, decoder, contract, preferred_element_type=jnp.float32)
    alive = (jnp.arange(atom_dev) < block_count[0] * BLOCK).astype(jnp.float32)
    summed = lax.psum(raw_gram, "width")
    norms = jnp.sqrt(jnp.diagonal(summed) + epsilon)
    weights = coherence_weights(summed, norms, norms, alive, alive)
    penalty = jnp.dot(weights, decoder, preferred_element_type=jnp.float32)
    decoder_grad = (fitted + penalty).astype(jnp.bfloat16)
    return (residual, encoder_grad, decoder_grad, bias_grad)


MESH = pl.DeviceIdType.MESH
CHUNK = 32
PLACES = 4


def gather_kernel(n, src_ref, out_ref, send_sem, recv_sem, own_sem):
    rows = src_ref.shape[0]
    chunks = rows // CHUNK
    line = n // PLACES
    me = lax.axis_index("atoms")
    across_width = lax.axis_index("width")
    core = lax.rem(me, 2)
    side = lax.rem(me // 2, 2)
    level = me // PLACES
    up, down = me + PLACES, me - PLACES
    across = me + 2 - 4 * side
    sibling = me + 1 - 2 * core
    has_up = level < line - 1
    has_down = level > 0

    barrier = pltpu.get_barrier_semaphore()

    def greet(device):
        pl.semaphore_signal(
            barrier, inc=1, device_id=(device, across_width), device_id_type=MESH
        )

    greet(across)
    greet(sibling)

    @pl.when(has_up)
    def _():
        greet(up)

    @pl.when(has_down)
    def _():
        greet(down)

    peers = 2 + has_up.astype(jnp.int32) + has_down.astype(jnp.int32)
    pl.semaphore_wait(barrier, peers)

    def piece(k):
        return pl.ds(pl.multiple_of(k * CHUNK, CHUNK), CHUNK)

    def copy(slot, k, way, device, own=False):
        here = src_ref.at[piece(k)] if own else out_ref.at[slot, piece(k)]
        return pltpu.make_async_remote_copy(
            src_ref=here,
            dst_ref=out_ref.at[slot, piece(k)],
            send_sem=send_sem.at[slot, k, way],
            recv_sem=recv_sem.at[slot, k],
            device_id=(device, across_width),
            device_id_type=MESH,
        )

    def arrived(slot, k):
        copy(slot, k, 0, sibling).wait_recv()

    def over_chunks(body):
        def step(k, carry):
            body(k)
            return carry

        lax.fori_loop(0, chunks, step, 0)

    own_copy = pltpu.make_async_copy(src_ref, out_ref.at[me], own_sem)
    own_copy.start()

    def spread(k, act):
        @pl.when(has_up)
        def _():
            act(copy(me, k, 0, up, True))

        @pl.when(has_down)
        def _():
            act(copy(me, k, 1, down, True))

        act(copy(me, k, 2, across, True))
        act(copy(me, k, 3, sibling, True))

    def pass_on(hop, k, act, wait):
        @pl.when(level >= hop)
        def _():
            slot = me - PLACES * hop
            if wait:
                arrived(slot, k)

            @pl.when(has_up)
            def _():
                act(copy(slot, k, 0, up))

            act(copy(slot, k, 2, across))
            act(copy(slot, k, 3, sibling))

        @pl.when(level + hop < line)
        def _():
            slot = me + PLACES * hop
            if wait:
                arrived(slot, k)

            @pl.when(has_down)
            def _():
                act(copy(slot, k, 1, down))

            act(copy(slot, k, 2, across))
            act(copy(slot, k, 3, sibling))

    def hand_over(hop, k, act, wait):
        if hop == 0:
            if wait:
                arrived(across, k)
            act(copy(across, k, 3, sibling))
            return

        @pl.when(level >= hop)
        def _():
            slot = across - PLACES * hop
            if wait:
                arrived(slot, k)
            act(copy(slot, k, 3, sibling))

        @pl.when(level + hop < line)
        def _():
            slot = across + PLACES * hop
            if wait:
                arrived(slot, k)
            act(copy(slot, k, 3, sibling))

    def start(c):
        c.start()

    def sent(c):
        c.wait_send()

    over_chunks(lambda k: spread(k, start))
    for hop in range(1, line + 1):

        def turn(k, hop=hop):
            if hop < line:
                pass_on(hop, k, start, True)
            hand_over(hop - 1, k, start, True)

        over_chunks(turn)

    def last(k):
        for place in range(n // 2):
            arrived(2 * place + 1 - core, k)

    over_chunks(last)

    def drain(k):
        spread(k, sent)
        for hop in range(line):
            if hop:
                pass_on(hop, k, sent, False)
            hand_over(hop, k, sent, False)

    over_chunks(drain)
    own_copy.wait()


def gathered(x, n, collective_id):
    rows, width = x.shape
    chunks = rows // CHUNK
    return pl.pallas_call(
        functools.partial(gather_kernel, n),
        out_shape=jax.ShapeDtypeStruct((n, rows, width), x.dtype),
        in_specs=[pl.BlockSpec(memory_space=pl.ANY)],
        out_specs=pl.BlockSpec(memory_space=pl.ANY),
        scratch_shapes=[
            pltpu.SemaphoreType.DMA((n, chunks, 4)),
            pltpu.SemaphoreType.DMA((n, chunks)),
            pltpu.SemaphoreType.DMA,
        ],
        compiler_params=pltpu.CompilerParams(collective_id=collective_id, has_side_effects=True),
        cost_estimate=pl.CostEstimate(
            flops=0, bytes_accessed=16 * n * rows * width, transcendentals=0
        ),
        name=f"gather_{collective_id}",
    )(x)


def decode_kernel(act_ref, dec_ref, tok_ref, bias_ref, out_ref, total):
    step = pl.program_id(0)
    width = tok_ref.shape[1]
    tile = min(width, 512)

    @pl.when(step == 0)
    def _():
        total[...] = jnp.broadcast_to(bias_ref[...], total.shape)

    for at in range(0, width, tile):
        cols = pl.ds(at, tile)
        term = jnp.dot(act_ref[0], dec_ref[0, :, cols], preferred_element_type=jnp.float32)
        total[:, cols] += term.astype(jnp.bfloat16).astype(jnp.float32)

    @pl.when(step == pl.num_programs(0) - 1)
    def _():
        for at in range(0, width, tile):
            cols = pl.ds(at, tile)
            out_ref[:, cols] = (total[:, cols] - tok_ref[:, cols].astype(jnp.float32)).astype(
                jnp.bfloat16
            )


def decode(acts, rows, tokens, dec_bias):
    n, atom_dev, width = rows.shape
    tok_dev = tokens.shape[0]
    return pl.pallas_call(
        decode_kernel,
        grid=(n,),
        out_shape=jax.ShapeDtypeStruct(tokens.shape, jnp.bfloat16),
        in_specs=[
            pl.BlockSpec((1, tok_dev, atom_dev), lambda o: (o, 0, 0)),
            pl.BlockSpec((1, atom_dev, width), lambda o: (o, 0, 0)),
            pl.BlockSpec((tok_dev, width), lambda o: (0, 0)),
            pl.BlockSpec((1, width), lambda o: (0, 0)),
        ],
        out_specs=pl.BlockSpec((tok_dev, width), lambda o: (0, 0)),
        scratch_shapes=[pltpu.VMEM((tok_dev, width), jnp.float32)],
        compiler_params=pltpu.CompilerParams(vmem_limit_bytes=32 * 1024 * 1024),
        name="decode",
    )(acts, rows, tokens, dec_bias[None, :])


def collected(tokens, dec_bias, encoder, enc_bias, decoder, atom_ids, block_count):
    tok_dev, width_shard = tokens.shape
    atom_dev = encoder.shape[0]
    owner_total = lax.axis_size("atoms")
    pick = atom_ids.shape[1]
    token_total = owner_total * tok_dev
    contract = (((1,), (1,)), ((), ()))
    contract_rows = (((0,), (0,)), ((), ()))
    wide = jnp.float32
    centered = (tokens.astype(wide) - dec_bias).astype(jnp.bfloat16)
    ids_all = lax.all_gather(atom_ids, "atoms", axis=0, tiled=True)
    raw_gram = lax.dot_general(decoder, decoder, contract, preferred_element_type=wide)
    summed = lax.psum(raw_gram, "width")
    centered_all = gathered(centered, owner_total, 1).reshape(token_total, width_shard)
    scores = lax.dot_general(centered_all, encoder, contract, preferred_element_type=wide)
    scores = lax.psum(scores.astype(jnp.bfloat16), "width").astype(wide)
    columns = lax.axis_index("atoms") * atom_dev + jnp.arange(atom_dev)[None, :]
    hit = functools.reduce(
        jnp.logical_or, [ids_all[:, k : k + 1] == columns for k in range(pick)]
    )
    act_table = jnp.where(hit, scores + enc_bias[None, :], 0.0).astype(jnp.bfloat16)
    acts = lax.all_to_all(
        act_table.reshape(owner_total, tok_dev, atom_dev), "atoms", split_axis=0, concat_axis=0, tiled=True
    )
    decoder_all = gathered(decoder, owner_total, 2)
    residual = decode(acts, decoder_all, tokens, dec_bias)
    back = lax.dot_general(
        residual,
        decoder_all.reshape(owner_total * atom_dev, width_shard),
        contract,
        preferred_element_type=wide,
    )
    slots = jnp.arange(owner_total * atom_dev)[None, :]
    picked = jnp.stack(
        [jnp.sum(jnp.where(atom_ids[:, k : k + 1] == slots, back, 0.0), axis=1) for k in range(pick)],
        axis=1,
    )
    dact = lax.psum(picked, "width") * loss_grad
    dact_all = lax.all_gather(dact, "atoms", axis=0, tiled=True)
    residual_all = gathered(residual, owner_total, 3).reshape(token_total, width_shard)
    dact_table = functools.reduce(
        jnp.add,
        [
            jnp.where(ids_all[:, k : k + 1] == columns, dact_all[:, k : k + 1], 0.0)
            for k in range(pick)
        ],
    )
    bias_grad = jnp.sum(dact_table, axis=0)
    encoder_grad = lax.dot_general(
        dact_table.astype(jnp.bfloat16), centered_all, contract_rows, preferred_element_type=wide
    ).astype(jnp.bfloat16)
    alive = (jnp.arange(atom_dev) < block_count[0] * BLOCK).astype(wide)
    norms = jnp.sqrt(jnp.diagonal(summed) + epsilon)
    weights = coherence_weights(summed, norms, norms, alive, alive)
    penalty = jnp.dot(weights, decoder, preferred_element_type=wide)
    fitted = (
        lax.dot_general(act_table, residual_all, contract_rows, preferred_element_type=wide)
        * loss_grad
    )
    decoder_grad = (fitted + penalty).astype(jnp.bfloat16)
    return (residual, encoder_grad, decoder_grad, bias_grad)


GATHER_BYTES = 32 * 1024 * 1024


def per_device(tokens, *others):
    owners = lax.axis_size("atoms")
    room = owners * tokens.size * tokens.dtype.itemsize <= GATHER_BYTES
    even = owners % PLACES == 0 and tokens.shape[0] % CHUNK == 0
    return (collected if room and even else dispatched)(tokens, *others)


def solution(mesh):
    in_specs = (
        P("atoms", "width"),
        P("width"),
        P("atoms", "width"),
        P("atoms"),
        P("atoms", "width"),
        P("atoms", None),
        P("atoms"),
    )
    out_specs = (P("atoms", "width"), P("atoms", "width"), P("atoms", "width"), P("atoms"))
    return jax.shard_map(
        per_device, mesh=mesh, in_specs=in_specs, out_specs=out_specs, check_vma=False
    )
```

```python
import functools

import jax
import jax.numpy as jnp
from jax import lax
from jax.experimental import pallas as pl
from jax.experimental.pallas import tpu as pltpu
from jax.sharding import PartitionSpec as P

BLOCK = 64


coherence = 128.0
loss_grad = 1.0 / 32.0
epsilon = 1e-06


def coherence_weights(raw_rows, norm_rows, norm_all, alive_rows, alive_all):
    row_total, extent = raw_rows.shape
    row_ids = jnp.arange(row_total)[:, None]
    col_ids = jnp.arange(extent)[None, :]
    norm_pair = norm_rows[:, None] * norm_all[None, :]
    cosine = raw_rows / norm_pair
    on_diagonal = row_ids == col_ids
    coupled = jnp.where(on_diagonal, 0.0, alive_rows[:, None] * alive_all[None, :] * cosine)
    spread = jnp.sum(coupled * cosine, axis=1)
    diag_term = jnp.where(on_diagonal, (spread / (norm_rows * norm_rows))[:, None], 0.0)
    return (4.0 * coherence * (coupled / norm_pair - diag_term)).astype(jnp.bfloat16)


def picked_pair(table, hit_a, hit_b):
    first_pick = jnp.sum(jnp.where(hit_a, table, 0.0), axis=1)
    second_pick = jnp.sum(jnp.where(hit_b, table, 0.0), axis=1)
    return (first_pick, second_pick)


def dispatched(tokens, dec_bias, encoder, enc_bias, decoder, atom_ids, block_count):
    tok_dev, width_shard = tokens.shape
    atom_dev = encoder.shape[0]
    owner_total = lax.axis_size("atoms")
    pair_total = atom_ids.shape[1] // 2
    capacity = 3 * tok_dev * pair_total // (2 * owner_total)
    slot_total = owner_total * capacity
    contract = (((1,), (1,)), ((), ()))
    contract_rows = (((0,), (0,)), ((), ()))
    centered = (tokens.astype(jnp.float32) - dec_bias).astype(jnp.bfloat16)
    pair_ids = atom_ids.reshape(tok_dev * pair_total, 2)
    owner_of = pair_ids[:, 0] // atom_dev
    local_atom = pair_ids % atom_dev
    member = (owner_of[:, None] == jnp.arange(owner_total)[None, :]).astype(jnp.int32)
    before = jnp.cumsum(member, axis=0) - member
    slot_of = owner_of * capacity + jnp.sum(before * member, axis=1)
    source_tok = jnp.arange(tok_dev * pair_total) // pair_total
    outgoing = (
        jnp.zeros((slot_total, width_shard), jnp.bfloat16).at[slot_of].set(centered[source_tok])
    )
    slot_tags = jnp.concatenate([local_atom, source_tok[:, None]], axis=1)
    tag_out = jnp.full((slot_total, 3), -1, jnp.int32).at[slot_of].set(slot_tags)
    incoming = lax.all_to_all(outgoing, "atoms", split_axis=0, concat_axis=0, tiled=True)
    tag_in = lax.all_to_all(tag_out, "atoms", split_axis=0, concat_axis=0, tiled=True)
    columns = jnp.arange(atom_dev)[None, :]
    hit_a = tag_in[:, 0:1] == columns
    hit_b = tag_in[:, 1:2] == columns
    scores = lax.dot_general(incoming, encoder, contract, preferred_element_type=jnp.float32)
    scores = lax.psum(scores.astype(jnp.bfloat16), "width").astype(jnp.float32)
    pre_a, pre_b = picked_pair(scores, hit_a, hit_b)
    bias_a, bias_b = picked_pair(enc_bias[None, :], hit_a, hit_b)
    act_a = (pre_a + bias_a).astype(jnp.bfloat16)
    act_b = (pre_b + bias_b).astype(jnp.bfloat16)
    zero_low = jnp.zeros((), jnp.bfloat16)
    act_table = jnp.where(hit_a, act_a[:, None], zero_low) + jnp.where(
        hit_b, act_b[:, None], zero_low
    )
    decoded = jnp.dot(act_table, decoder, preferred_element_type=jnp.float32).astype(jnp.bfloat16)
    returned = lax.all_to_all(decoded, "atoms", split_axis=0, concat_axis=0, tiled=True)
    own_terms = returned[slot_of].reshape(tok_dev, pair_total, width_shard).astype(jnp.float32)
    residual = (jnp.sum(own_terms, axis=1) + dec_bias - tokens.astype(jnp.float32)).astype(
        jnp.bfloat16
    )
    token_of_slot = jnp.maximum(tag_in[:, 2], 0)
    piece = lax.all_gather(residual, "atoms", axis=0, tiled=True)
    rows = piece.shape[0]
    src_count = rows // tok_dev
    offset = jnp.arange(src_count * capacity) // capacity * tok_dev
    picked = piece[token_of_slot + offset]
    back_scores = lax.dot_general(picked, decoder, contract, preferred_element_type=jnp.float32)
    back_scores = lax.psum(back_scores.astype(jnp.bfloat16), "width").astype(jnp.float32)
    grad_a, grad_b = picked_pair(back_scores, hit_a, hit_b)
    dact_a = grad_a * loss_grad
    dact_b = grad_b * loss_grad
    dact_table = jnp.where(hit_a, dact_a[:, None], 0.0) + jnp.where(hit_b, dact_b[:, None], 0.0)
    bias_grad = jnp.sum(dact_table, axis=0)
    encoder_grad = lax.dot_general(
        dact_table.astype(jnp.bfloat16), incoming, contract_rows, preferred_element_type=jnp.float32
    ).astype(jnp.bfloat16)
    fitted = (
        lax.dot_general(act_table, picked, contract_rows, preferred_element_type=jnp.float32)
        * loss_grad
    )
    raw_gram = lax.dot_general(decoder, decoder, contract, preferred_element_type=jnp.float32)
    alive = (jnp.arange(atom_dev) < block_count[0] * BLOCK).astype(jnp.float32)
    summed = lax.psum(raw_gram, "width")
    norms = jnp.sqrt(jnp.diagonal(summed) + epsilon)
    weights = coherence_weights(summed, norms, norms, alive, alive)
    penalty = jnp.dot(weights, decoder, preferred_element_type=jnp.float32)
    decoder_grad = (fitted + penalty).astype(jnp.bfloat16)
    return (residual, encoder_grad, decoder_grad, bias_grad)


MESH = pl.DeviceIdType.MESH
CHUNK = 32
HEAD = 16
PLACES = 4


def gather_kernel(n, tagged, *refs):
    if tagged:
        src_ref, tag_ref, out_ref, tags_ref, send_sem, recv_sem, own_sem = refs
    else:
        src_ref, out_ref, send_sem, recv_sem, own_sem = refs
    rows = src_ref.shape[0]
    chunks = (rows - HEAD) // CHUNK
    rest = rows - HEAD - chunks * CHUNK
    line = n // PLACES
    me = lax.axis_index("atoms")
    across_width = lax.axis_index("width")
    core = lax.rem(me, 2)
    side = lax.rem(me // 2, 2)
    level = me // PLACES
    up, down = me + PLACES, me - PLACES
    across = me + 2 - 4 * side
    sibling = me + 1 - 2 * core
    has_up = level < line - 1
    has_down = level > 0

    barrier = pltpu.get_barrier_semaphore()

    def greet(device):
        pl.semaphore_signal(
            barrier, inc=1, device_id=(device, across_width), device_id_type=MESH
        )

    greet(across)
    greet(sibling)

    @pl.when(has_up)
    def _():
        greet(up)

    @pl.when(has_down)
    def _():
        greet(down)

    peers = 2 + has_up.astype(jnp.int32) + has_down.astype(jnp.int32)
    pl.semaphore_wait(barrier, peers)

    TAG, FIRST, LAST = "tag", "first", "last"

    def piece(k):
        if isinstance(k, str):
            return pl.ds(0, HEAD) if k == FIRST else pl.ds(rows - rest, rest)
        return pl.ds(pl.multiple_of(HEAD + k * CHUNK, HEAD), CHUNK)

    def place(k):
        return {TAG: chunks + 2, FIRST: chunks, LAST: chunks + 1}[k] if isinstance(k, str) else k

    def copy(slot, k, way, device, own=False):
        if k == TAG if isinstance(k, str) else False:
            here = tag_ref if own else tags_ref.at[slot]
            there = tags_ref.at[slot]
        else:
            here = src_ref.at[piece(k)] if own else out_ref.at[slot, piece(k)]
            there = out_ref.at[slot, piece(k)]
        return pltpu.make_async_remote_copy(
            src_ref=here,
            dst_ref=there,
            send_sem=send_sem.at[slot, place(k), way],
            recv_sem=recv_sem.at[slot, place(k)],
            device_id=(device, across_width),
            device_id_type=MESH,
        )

    def arrived(slot, k):
        copy(slot, k, 0, sibling).wait_recv()

    def over_chunks(body):
        if tagged:
            body(TAG)
        body(FIRST)

        def step(k, carry):
            body(k)
            return carry

        lax.fori_loop(0, chunks, step, 0)
        if rest:
            body(LAST)

    own_copies = [pltpu.make_async_copy(src_ref, out_ref.at[me], own_sem.at[0])]
    if tagged:
        own_copies.append(pltpu.make_async_copy(tag_ref, tags_ref.at[me], own_sem.at[1]))
    for c in own_copies:
        c.start()

    def early(k):
        return isinstance(k, str) and k == FIRST

    def spread(slot, k, act, own):
        @pl.when(has_up)
        def _():
            act(copy(slot, k, 0, up, own))

        @pl.when(has_down)
        def _():
            act(copy(slot, k, 1, down, own))

        if own:
            act(copy(slot, k, 2, across, own))
        act(copy(slot, k, 3, sibling, own))

    def pass_on(hop, k, act, wait):
        columns = (me, across) if early(k) else (me,)

        @pl.when(level >= hop)
        def _():
            for column in columns:
                slot = column - PLACES * hop
                if wait:
                    arrived(slot, k)

                @pl.when(has_up)
                def _():
                    act(copy(slot, k, 0, up))

                if not early(k):
                    act(copy(slot, k, 2, across))
                act(copy(slot, k, 3, sibling))

        @pl.when(level + hop < line)
        def _():
            for column in columns:
                slot = column + PLACES * hop
                if wait:
                    arrived(slot, k)

                @pl.when(has_down)
                def _():
                    act(copy(slot, k, 1, down))

                if not early(k):
                    act(copy(slot, k, 2, across))
                act(copy(slot, k, 3, sibling))

    def hand_over(hop, k, act, wait):
        if early(k):
            return
        if hop == 0:
            if wait:
                arrived(across, k)
            act(copy(across, k, 3, sibling))
            return

        @pl.when(level >= hop)
        def _():
            slot = across - PLACES * hop
            if wait:
                arrived(slot, k)
            act(copy(slot, k, 3, sibling))

        @pl.when(level + hop < line)
        def _():
            slot = across + PLACES * hop
            if wait:
                arrived(slot, k)
            act(copy(slot, k, 3, sibling))

    def start(c):
        c.start()

    def sent(c):
        c.wait_send()

    over_chunks(lambda k: spread(me, k, start, True))
    arrived(across, FIRST)
    spread(across, FIRST, start, False)
    for hop in range(1, line + 1):

        def turn(k, hop=hop):
            if hop < line:
                pass_on(hop, k, start, True)
            hand_over(hop - 1, k, start, True)

        over_chunks(turn)

    def last(k):
        for spot in range(n // 2):
            arrived(2 * spot + 1 - core, k)

    over_chunks(last)

    def drain(k):
        spread(me, k, sent, True)
        if early(k):
            spread(across, k, sent, False)
        for hop in range(line):
            if hop:
                pass_on(hop, k, sent, False)
            hand_over(hop, k, sent, False)

    over_chunks(drain)
    for c in own_copies:
        c.wait()


def gathered(x, n, collective_id, tag=None):
    rows, width = x.shape
    chunks = (rows - HEAD) // CHUNK + 3
    arrays = [x] if tag is None else [x, tag]
    anywhere = pl.BlockSpec(memory_space=pl.ANY)
    out = pl.pallas_call(
        functools.partial(gather_kernel, n, tag is not None),
        out_shape=[jax.ShapeDtypeStruct((n, *a.shape), a.dtype) for a in arrays],
        in_specs=[anywhere] * len(arrays),
        out_specs=[anywhere] * len(arrays),
        scratch_shapes=[
            pltpu.SemaphoreType.DMA((n, chunks, 4)),
            pltpu.SemaphoreType.DMA((n, chunks)),
            pltpu.SemaphoreType.DMA((2,)),
        ],
        compiler_params=pltpu.CompilerParams(collective_id=collective_id, has_side_effects=True),
        cost_estimate=pl.CostEstimate(
            flops=0, bytes_accessed=16 * n * rows * width, transcendentals=0
        ),
        name=f"gather_{collective_id}",
    )(*arrays)
    return out[0] if tag is None else out


def decode_kernel(act_ref, dec_ref, tok_ref, bias_ref, out_ref, total):
    step = pl.program_id(0)
    width = tok_ref.shape[1]
    tile = min(width, 512)

    @pl.when(step == 0)
    def _():
        total[...] = jnp.broadcast_to(bias_ref[...], total.shape)

    for at in range(0, width, tile):
        cols = pl.ds(at, tile)
        term = jnp.dot(act_ref[0], dec_ref[0, :, cols], preferred_element_type=jnp.float32)
        total[:, cols] += term.astype(jnp.bfloat16).astype(jnp.float32)

    @pl.when(step == pl.num_programs(0) - 1)
    def _():
        for at in range(0, width, tile):
            cols = pl.ds(at, tile)
            out_ref[:, cols] = (total[:, cols] - tok_ref[:, cols].astype(jnp.float32)).astype(
                jnp.bfloat16
            )


def decode(acts, rows, tokens, dec_bias):
    n, atom_dev, width = rows.shape
    tok_dev = tokens.shape[0]
    return pl.pallas_call(
        decode_kernel,
        grid=(n,),
        out_shape=jax.ShapeDtypeStruct(tokens.shape, jnp.bfloat16),
        in_specs=[
            pl.BlockSpec((1, tok_dev, atom_dev), lambda o: (o, 0, 0)),
            pl.BlockSpec((1, atom_dev, width), lambda o: (o, 0, 0)),
            pl.BlockSpec((tok_dev, width), lambda o: (0, 0)),
            pl.BlockSpec((1, width), lambda o: (0, 0)),
        ],
        out_specs=pl.BlockSpec((tok_dev, width), lambda o: (0, 0)),
        scratch_shapes=[pltpu.VMEM((tok_dev, width), jnp.float32)],
        compiler_params=pltpu.CompilerParams(vmem_limit_bytes=32 * 1024 * 1024),
        name="decode",
    )(acts, rows, tokens, dec_bias[None, :])


def collected(tokens, dec_bias, encoder, enc_bias, decoder, atom_ids, block_count):
    tok_dev, width_shard = tokens.shape
    atom_dev = encoder.shape[0]
    owner_total = lax.axis_size("atoms")
    pick = atom_ids.shape[1]
    token_total = owner_total * tok_dev
    contract = (((1,), (1,)), ((), ()))
    wide = jnp.float32
    centered = (tokens.astype(wide) - dec_bias).astype(jnp.bfloat16)
    raw_gram = lax.dot_general(decoder, decoder, contract, preferred_element_type=wide)
    summed = lax.psum(raw_gram, "width")
    centered_all, ids_all = gathered(centered, owner_total, 1, atom_ids.T)
    centered_all = centered_all.reshape(token_total, width_shard)
    scores = lax.dot_general(encoder, centered_all, contract, preferred_element_type=wide)
    me = lax.axis_index("atoms")
    first_ids, second_ids = ids_all[:, 0::2, :], ids_all[:, 1::2, :]
    owned = first_ids // atom_dev == me
    base = me * atom_dev

    def owned_row(values, blank):
        kept = jnp.where(owned, values, blank)
        kept = jnp.max(kept, axis=1) if blank else jnp.sum(kept, axis=1)
        return lax.optimization_barrier(kept.reshape(1, token_total))

    atoms = jnp.arange(atom_dev)
    hit_a = owned_row(first_ids - base, -1) == atoms[:, None]
    hit_b = owned_row(second_ids - base, -1) == atoms[:, None]

    def picked_row(table, hit):
        return jnp.sum(jnp.where(hit, table, 0.0), axis=0)

    pre = lax.psum(jnp.stack([picked_row(scores, hit_a), picked_row(scores, hit_b)]), "width")
    biases = jnp.stack(
        [picked_row(enc_bias[:, None], hit_a), picked_row(enc_bias[:, None], hit_b)]
    )
    act_pair = (pre + biases).astype(jnp.bfloat16).astype(wide)
    decoder_all, acts_all = gathered(
        decoder, owner_total, 2, act_pair.reshape(2 * owner_total, tok_dev)
    )
    act_a = lax.dynamic_index_in_dim(acts_all, me, 1, keepdims=False)
    act_b = lax.dynamic_index_in_dim(acts_all, owner_total + me, 1, keepdims=False)
    first, second = atom_ids[:, 0::2].T, atom_ids[:, 1::2].T
    of_owner = first[None] // atom_dev == jnp.arange(owner_total)[:, None, None]
    local_a = jnp.max(jnp.where(of_owner, first[None] % atom_dev, -1), axis=1)
    local_b = jnp.max(jnp.where(of_owner, second[None] % atom_dev, -1), axis=1)
    acts = (
        jnp.where(local_a[:, :, None] == atoms, act_a[:, :, None], 0.0)
        + jnp.where(local_b[:, :, None] == atoms, act_b[:, :, None], 0.0)
    ).astype(jnp.bfloat16)
    residual = decode(acts, decoder_all, tokens, dec_bias)
    back = lax.dot_general(
        residual,
        decoder_all.reshape(owner_total * atom_dev, width_shard),
        contract,
        preferred_element_type=wide,
    )
    slots = jnp.arange(owner_total * atom_dev)[None, :]
    picked = jnp.stack(
        [jnp.sum(jnp.where(atom_ids[:, k : k + 1] == slots, back, 0.0), axis=1) for k in range(pick)]
    )
    dact = lax.psum(picked, "width") * loss_grad
    residual_all, dact_all = gathered(residual, owner_total, 3, dact)
    residual_all = residual_all.reshape(token_total, width_shard)
    dact_a = owned_row(dact_all[:, 0::2, :], 0.0)
    dact_b = owned_row(dact_all[:, 1::2, :], 0.0)
    dact_table = jnp.where(hit_a, dact_a, 0.0) + jnp.where(hit_b, dact_b, 0.0)
    bias_grad = jnp.sum(dact_table, axis=1)
    dact_low = lax.optimization_barrier(dact_table.astype(jnp.bfloat16))
    encoder_grad = jnp.dot(dact_low, centered_all, preferred_element_type=wide).astype(
        jnp.bfloat16
    )
    act_table = jnp.where(hit_a, act_pair[0:1], 0.0) + jnp.where(hit_b, act_pair[1:2], 0.0)
    act_table = lax.optimization_barrier(act_table.astype(jnp.bfloat16))
    alive = (jnp.arange(atom_dev) < block_count[0] * BLOCK).astype(wide)
    norms = jnp.sqrt(jnp.diagonal(summed) + epsilon)
    weights = coherence_weights(summed, norms, norms, alive, alive)
    penalty = jnp.dot(weights, decoder, preferred_element_type=wide)
    fitted = jnp.dot(act_table, residual_all, preferred_element_type=wide) * loss_grad
    decoder_grad = (fitted + penalty).astype(jnp.bfloat16)
    return (residual, encoder_grad, decoder_grad, bias_grad)


GATHER_BYTES = 32 * 1024 * 1024


def per_device(tokens, *others):
    owners = lax.axis_size("atoms")
    room = owners * tokens.size * tokens.dtype.itemsize <= GATHER_BYTES
    even = owners % PLACES == 0 and tokens.shape[0] % HEAD == 0
    return (collected if room and even else dispatched)(tokens, *others)


def solution(mesh):
    in_specs = (
        P("atoms", "width"),
        P("width"),
        P("atoms", "width"),
        P("atoms"),
        P("atoms", "width"),
        P("atoms", None),
        P("atoms"),
    )
    out_specs = (P("atoms", "width"), P("atoms", "width"), P("atoms", "width"), P("atoms"))
    return jax.shard_map(
        per_device, mesh=mesh, in_specs=in_specs, out_specs=out_specs, check_vma=False
    )
```
